32 devices in a mesh: gx: 2 (over x), gy: 4 (over y, core), gz: 4 (over z).
Axes of the slice: x: 2, y: 2, z: 4, core: 2. Of those that a mesh axis runs over, the one named last changes fastest.
Arguments:
- thermal_state_values: float32 [32, 128, 512], P('gx', 'gy', 'gz'), may hold values from -6 to 6
- flow_speed_components: float32 [3, 32, 128, 512], P(None, 'gx', 'gy', 'gz'), may hold values from -14 to 14
- thermal_diffusivity_coefficient: float32 [32, 128, 512], P('gx', 'gy', 'gz'), may hold values from 0.1 to 3
- specific_volume: float32 [32, 128, 512], P('gx', 'gy', 'gz'), may hold values from 0.5 to 2
- lower_level_helmholtz_offset: float32 [4, 16, 64], P('gx', 'gy', 'gz'), may hold values from 0.5 to 4
Outputs:
- updated_thermal_state: float32 [32, 128, 512], P('gx', 'gy', 'gz')
- pressure_iterate_values: float32 [32, 128, 512], P('gx', 'gy', 'gz')
- pressure_residual: float32 [32, 128, 512], P('gx', 'gy', 'gz')
The draws below stay inside these ranges and needn't reach their ends.
All inputs are finite; a program needn't handle non-finite values.
Results may differ from the reference program's by a relative error of at most 0.0003.
Values sent between devices are 32-bit elements; how exact they have to be, the bound alone decides.
A program may use at most 128 MiB of HBM per device.

```python
import math
import jax
import jax.numpy as jnp
from jax import lax

PITERS = 2
SMOOTH = 3
CHEB_C = 8
POINTS_ALONG_X = 32
POINTS_ALONG_Y = 128
POINTS_ALONG_Z = 512
ELEMENTS_FIRST = 4
ELEMENTS_SECOND = 16
ELEMENTS_THIRD = 64


def node_coord(count):
    node_ids = jnp.arange(count)
    local_pt = (node_ids % 8).astype(jnp.float32)
    element_no = (node_ids // 8).astype(jnp.float32)
    return element_no + 0.5 - 0.5 * jnp.cos(math.pi * local_pt / 7.0)


def draw_flow_speed_components(key, part):
    noise_key, phase_key = jax.random.split(jax.random.fold_in(key, 17))
    coords = (node_coord(POINTS_ALONG_X)[:, None, None], node_coord(POINTS_ALONG_Y)[None, :, None], node_coord(POINTS_ALONG_Z)[None, None, :])
    phases = jax.random.uniform(phase_key, (6,), jnp.float32, 0.0, 2.0 * math.pi)
    noise = 2.0 * jax.random.truncated_normal(noise_key, -4.0, 4.0, (3, POINTS_ALONG_X, POINTS_ALONG_Y, POINTS_ALONG_Z), jnp.float32)
    amplitude = 4.0
    wave_num = 2.0 * math.pi / 6.0
    components = []
    for direction_index in range(3):
        along = jnp.sin(wave_num * coords[direction_index] + phases[direction_index])
        across = 1.0 + 0.5 * jnp.sin(wave_num * coords[(direction_index + 1) % 3] + phases[direction_index + 3])
        components.append(jnp.broadcast_to(amplitude * along * across, (POINTS_ALONG_X, POINTS_ALONG_Y, POINTS_ALONG_Z)))
    return noise + jnp.stack(components)


def block_scale(rng, dims, cuts, smallest, top_value):
    def one(dim, shards_of):
        heights = jax.random.uniform(jax.random.fold_in(jax.random.fold_in(rng, 6), dim), (shards_of,), jnp.float32, smallest / len(cuts), top_value / len(cuts))
        return jnp.repeat(jnp.exp(heights), dims[dim] // shards_of).reshape((-1,) + (1,) * (len(dims) - dim - 1))

    gain = one(*cuts[0])
    for cut in cuts[1:]:
        gain = gain * one(*cut)
    return gain


def gaussian(rng, dims, deviation, bound, pieces=(), kind=jnp.bfloat16):
    entries = deviation * jax.random.normal(rng, dims, jnp.float32)
    if pieces:
        entries = entries * block_scale(rng, dims, pieces, -0.22, 0.18)
    return jnp.clip(entries, -bound, bound).astype(kind)


def setup_inputs(seed: int = 0) -> dict:
    seeds = jax.random.split(jax.random.key(seed), 6)
    return {
        "thermal_state_values": gaussian(seeds[0], (POINTS_ALONG_X, POINTS_ALONG_Y, POINTS_ALONG_Z), 1.0, 6.0, ((0, 2), (1, 4), (2, 4)), jnp.float32),
        "flow_speed_components": draw_flow_speed_components(jax.random.fold_in(seeds[5], 71), 0),
        "thermal_diffusivity_coefficient": jnp.clip(jnp.exp(math.log(3.0) - 3.4011974 * jax.random.uniform(seeds[2], (POINTS_ALONG_X, POINTS_ALONG_Y, POINTS_ALONG_Z), jnp.float32) ** block_scale(seeds[2], (POINTS_ALONG_X, POINTS_ALONG_Y, POINTS_ALONG_Z), ((0, 2), (1, 4), (2, 4)), -0.2, 0.2)), 0.1, 3.0),
        "specific_volume": jnp.clip(jnp.exp(math.log(2.0) - 1.3862944 * jax.random.uniform(seeds[3], (POINTS_ALONG_X, POINTS_ALONG_Y, POINTS_ALONG_Z), jnp.float32) ** block_scale(seeds[3], (POINTS_ALONG_X, POINTS_ALONG_Y, POINTS_ALONG_Z), ((0, 2), (1, 4), (2, 4)), -0.2, 0.2)), 0.5, 2.0),
        "lower_level_helmholtz_offset": jnp.clip(jnp.exp(math.log(4.0) - 2.0794415 * jax.random.uniform(seeds[4], (ELEMENTS_FIRST, ELEMENTS_SECOND, ELEMENTS_THIRD), jnp.float32) ** block_scale(seeds[4], (ELEMENTS_FIRST, ELEMENTS_SECOND, ELEMENTS_THIRD), ((0, 2), (1, 4), (2, 4)), -0.2, 0.2)), 0.5, 4.0),
    }


CLOCK_STEP_SIZE = 0.0002
HELM_SHIFT = 1.0
FINE_LOW = 0.25
FINE_HIGH = 3.0
COARSE_LOW = 0.07
COARSE_HIGH = 2.0
GLL_POINTS = (-1.0, -0.8717401485096066, -0.5917001814331423, -0.2092992179024789, 0.0, 0.2092992179024789, 0.5917001814331423, 0.8717401485096066, 1.0)


def legendre_seven(point):
    p_prev = 1.0
    p_cur = point
    for order_k in range(1, 7):
        p_next = ((2.0 * order_k + 1.0) * point * p_cur - order_k * p_prev) / (order_k + 1.0)
        p_prev = p_cur
        p_cur = p_next
    return p_cur


def gll_tables():
    degree_n = 7
    points = list(GLL_POINTS[:4] + GLL_POINTS[5:])
    legend = [legendre_seven(point) for point in points]
    weights = [2.0 / (degree_n * (degree_n + 1) * value * value) for value in legend]
    derivs = []
    for row_no in range(8):
        row_vals = []
        for col_no in range(8):
            if row_no != col_no:
                row_vals.append(legend[row_no] / (legend[col_no] * (points[row_no] - points[col_no])))
            else:
                row_vals.append(0.0)
        derivs.append(row_vals)
    derivs[0][0] = -degree_n * (degree_n + 1) / 4.0
    derivs[7][7] = degree_n * (degree_n + 1) / 4.0
    return jnp.asarray(derivs, jnp.float32), jnp.asarray(weights, jnp.float32)


def weight_cube(weights):
    return weights[:, None, None] * weights[None, :, None] * weights[None, None, :]


def pair_pass(padded, direction_index):
    extent = padded.shape[direction_index]
    zero_rim = jnp.zeros_like(lax.slice_in_dim(padded, 0, 1, axis=direction_index))
    shifted_up = jnp.concatenate([lax.slice_in_dim(padded, 1, extent, axis=direction_index), zero_rim], axis=direction_index)
    shifted_down = jnp.concatenate([zero_rim, lax.slice_in_dim(padded, 0, extent - 1, axis=direction_index)], axis=direction_index)
    position = lax.broadcasted_iota(jnp.int32, padded.shape, direction_index) % 8
    return padded + jnp.where(position == 0, shifted_up, 0.0) + jnp.where(position == 1, shifted_down, 0.0)


def assemble(values):
    padded = jnp.pad(values, 1)
    for direction_index in range(3):
        padded = pair_pass(padded, direction_index)
    return padded[1:-1, 1:-1, 1:-1]


def apply_derivative_matrix(values, small_t, direction_index):
    full_shape = values.shape
    blocks = values.reshape(full_shape[:direction_index] + (full_shape[direction_index] // 8, 8) + full_shape[direction_index + 1:])
    result = jnp.tensordot(blocks, small_t, axes=([direction_index + 1], [1]), precision=lax.Precision.HIGHEST)
    return jnp.moveaxis(result, -1, direction_index + 1).reshape(full_shape)


def stencil(padded, shift_c):
    centre = padded[1:-1, 1:-1, 1:-1]
    beside_all = padded[2:, 1:-1, 1:-1] + padded[:-2, 1:-1, 1:-1]
    beside_all = beside_all + padded[1:-1, 2:, 1:-1] + padded[1:-1, :-2, 1:-1]
    beside_all = beside_all + padded[1:-1, 1:-1, 2:] + padded[1:-1, 1:-1, :-2]
    return (6.0 + shift_c) * centre - beside_all


def chebyshev(equation_misfit, apply_fn, inv_diag, low_end, high_end, sweeps, keep_resid):
    centre = 0.5 * (high_end + low_end)
    half_span = 0.5 * (high_end - low_end)
    span_ratio = centre / half_span
    rho_old = 1.0 / span_ratio
    direction = (equation_misfit * inv_diag) * (1.0 / centre)
    solution = direction
    for sweep_no in range(1, sweeps):
        equation_misfit = equation_misfit - apply_fn(direction)
        rho_new = 1.0 / (2.0 * span_ratio - rho_old)
        direction = (rho_new * rho_old) * direction + (2.0 * rho_new / half_span) * (equation_misfit * inv_diag)
        solution = solution + direction
        rho_old = rho_new
    if keep_resid:
        equation_misfit = equation_misfit - apply_fn(direction)
    return solution, equation_misfit


def reference(thermal_state_values, flow_speed_components, thermal_diffusivity_coefficient, specific_volume, lower_level_helmholtz_offset):
    derivs, weights = gll_tables()
    interpolation_apply = derivs
    adjoint_interpolation = derivs.T
    square_back = (derivs * derivs).T
    cube_w = weight_cube(weights)
    count_x, count_y, count_z = lower_level_helmholtz_offset.shape
    quadrature_coefficient = jnp.tile(cube_w, (count_x, count_y, count_z))
    quadrature_lumped_matrix = assemble(quadrature_coefficient)
    partial_derivative_stack = [apply_derivative_matrix(thermal_state_values, interpolation_apply, direction_index) for direction_index in range(3)]
    advect = flow_speed_components[0] * partial_derivative_stack[0] + flow_speed_components[1] * partial_derivative_stack[1] + flow_speed_components[2] * partial_derivative_stack[2]
    diffuse = apply_derivative_matrix(quadrature_coefficient * thermal_diffusivity_coefficient * partial_derivative_stack[0], adjoint_interpolation, 0)
    diffuse = diffuse + apply_derivative_matrix(quadrature_coefficient * thermal_diffusivity_coefficient * partial_derivative_stack[1], adjoint_interpolation, 1)
    diffuse = diffuse + apply_derivative_matrix(quadrature_coefficient * thermal_diffusivity_coefficient * partial_derivative_stack[2], adjoint_interpolation, 2)
    volumetric_source_strength = assemble(-(quadrature_coefficient * advect) - diffuse)
    updated_thermal_state = thermal_state_values + CLOCK_STEP_SIZE * volumetric_source_strength / quadrature_lumped_matrix
    boundary_heat_outflow = apply_derivative_matrix(quadrature_coefficient * flow_speed_components[0], adjoint_interpolation, 0) + apply_derivative_matrix(quadrature_coefficient * flow_speed_components[1], adjoint_interpolation, 1)
    boundary_heat_outflow = boundary_heat_outflow + apply_derivative_matrix(quadrature_coefficient * (flow_speed_components[2] + updated_thermal_state), adjoint_interpolation, 2)
    right_side = assemble(boundary_heat_outflow)
    coef_w = quadrature_coefficient * specific_volume
    jacobi = assemble(apply_derivative_matrix(coef_w, square_back, 0) + apply_derivative_matrix(coef_w, square_back, 1) + apply_derivative_matrix(coef_w, square_back, 2) + HELM_SHIFT * quadrature_coefficient)
    inv_jac = 1.0 / jacobi

    def apply_fine(values):
        local_k = apply_derivative_matrix(coef_w * apply_derivative_matrix(values, interpolation_apply, 0), adjoint_interpolation, 0)
        local_k = local_k + apply_derivative_matrix(coef_w * apply_derivative_matrix(values, interpolation_apply, 1), adjoint_interpolation, 1)
        local_k = local_k + apply_derivative_matrix(coef_w * apply_derivative_matrix(values, interpolation_apply, 2), adjoint_interpolation, 2)
        return assemble(local_k + HELM_SHIFT * quadrature_coefficient * values)

    def apply_coarse(values):
        return stencil(jnp.pad(values, 1), lower_level_helmholtz_offset)

    coarse_inv = 1.0 / (6.0 + lower_level_helmholtz_offset)
    pressure_iterate_values = jnp.zeros_like(thermal_state_values)
    equation_misfit = right_side
    for iter_no in range(PITERS):
        smooth, resid_s = chebyshev(equation_misfit, apply_fine, inv_jac, FINE_LOW, FINE_HIGH, SMOOTH, True)
        coarse_r = (quadrature_coefficient * resid_s).reshape(count_x, 8, count_y, 8, count_z, 8).sum(axis=(1, 3, 5)) / 8.0
        correct, unused = chebyshev(coarse_r, apply_coarse, coarse_inv, COARSE_LOW, COARSE_HIGH, CHEB_C, False)
        expanded = jnp.repeat(jnp.repeat(jnp.repeat(correct, 8, 0), 8, 1), 8, 2)
        prolong = assemble(quadrature_coefficient * expanded) / quadrature_lumped_matrix
        pressure_iterate_values = pressure_iterate_values + smooth + prolong
        equation_misfit = resid_s - apply_fine(prolong)
    return updated_thermal_state, pressure_iterate_values, equation_misfit
```

```python
import functools
import itertools

import jax
import jax.numpy as jnp
import numpy as np
from jax import lax
from jax.experimental import pallas as pl
from jax.experimental.pallas import tpu as pltpu
from jax.sharding import PartitionSpec as P

PITERS = 2
SMOOTH = 3
CHEB_C = 8
CLOCK_STEP_SIZE = 0.0002
HELM_SHIFT = 1.0
FINE_LOW = 0.25
FINE_HIGH = 3.0
COARSE_LOW = 0.07
COARSE_HIGH = 2.0
GLL_POINTS = (
    -1.0,
    -0.8717401485096066,
    -0.5917001814331423,
    -0.2092992179024789,
    0.2092992179024789,
    0.5917001814331423,
    0.8717401485096066,
    1.0,
)
MESH = pl.DeviceIdType.MESH
HIGHEST = lax.Precision.HIGHEST
F32 = jnp.float32
OFFSETS = [o for o in itertools.product((-1, 0, 1), repeat=3) if o != (0, 0, 0)]
SLOT_OF = {o: n for n, o in enumerate(OFFSETS)}


def legendre_seven(point):
    p_prev = 1.0
    p_cur = point
    for order_k in range(1, 7):
        p_next = ((2.0 * order_k + 1.0) * point * p_cur - order_k * p_prev) / (order_k + 1.0)
        p_prev = p_cur
        p_cur = p_next
    return p_cur


def gll_tables():
    points = GLL_POINTS
    legend = [legendre_seven(point) for point in points]
    weights = [2.0 / (56.0 * value * value) for value in legend]
    derivs = np.zeros((8, 8))
    for i in range(8):
        for a in range(8):
            if i != a:
                derivs[i, a] = legend[i] / (legend[a] * (points[i] - points[a]))
    derivs[0, 0] = -14.0
    derivs[7, 7] = 14.0
    return derivs.astype(np.float32), np.asarray(weights, np.float32)


def dot(a, b, dims=((1,), (0,))):
    return lax.dot_general(a, b, (dims, ((), ())), precision=HIGHEST, preferred_element_type=F32)


def fine_coefficients():
    centre = 0.5 * (FINE_HIGH + FINE_LOW)
    half = 0.5 * (FINE_HIGH - FINE_LOW)
    ratio = centre / half
    rho = 1.0 / ratio
    steps = []
    for _ in range(1, SMOOTH):
        new = 1.0 / (2.0 * ratio - rho)
        steps.append((new * rho, 2.0 * new / half))
        rho = new
    return 1.0 / centre, steps


def kernel(
    sizes,
    blocks,
    temp_ref,
    flow_ref,
    cond_ref,
    vol_ref,
    off_ref,
    gz_ref,
    ky_ref,
    wyz_ref,
    wcol_ref,
    wrow_ref,
    newt_ref,
    press_ref,
    resid_ref,
    weight,
    coef,
    q,
    direc,
    part,
    ysend,
    zsend,
    xrecv,
    yrecv,
    zrecv,
    place,
    csend,
    cgrid,
    padded,
    pz,
    pxy,
    restr,
    send_sem,
    recv_sem,
    gsend_sem,
    grecv_sem,
):
    derivs, weights = gll_tables()
    nx, ny, nz = sizes
    bx, by, bz = blocks
    lx, ly, lz = 8 * bx, 8 * by, 8 * bz
    rows = 8 * ly
    devices = nx * ny * nz
    grid_x, grid_y, grid_z = nx * bx, ny * by, nz * bz
    ix, iy, iz = lax.axis_index("gx"), lax.axis_index("gy"), lax.axis_index("gz")
    me = (ix * ny + iy) * nz + iz

    def coords(linear):
        return (linear // (ny * nz), (linear // nz) % ny, linear % nz)

    xrecv[...] = jnp.zeros(xrecv.shape, F32)
    yrecv[...] = jnp.zeros(yrecv.shape, F32)
    zrecv[...] = jnp.zeros(zrecv.shape, F32)

    barrier = pltpu.get_barrier_semaphore()

    def greet(n, carry):
        pl.semaphore_signal(
            barrier, inc=1, device_id=coords(lax.rem(me + n, devices)), device_id_type=MESH
        )
        return carry

    lax.fori_loop(1, devices, greet, 0)

    lane = lax.broadcasted_iota(jnp.int32, (rows, lz), 1)
    row_y = lax.broadcasted_iota(jnp.int32, (rows, lz), 0) % ly
    z_up = (lane % 8 == 7) & (lane < lz - 1)
    z_down = (lane % 8 == 0) & (lane > 0)
    y_up = (row_y % 8 == 7) & (row_y < ly - 1)
    y_down = (row_y % 8 == 0) & (row_y > 0)

    for x in range(lx):
        weight[x] = wyz_ref[...] * float(weights[x % 8])
    coef[...] = weight[...] * vol_ref[...]

    def share(node, elements, element):
        owner = node // 8
        local = node % 8
        low = (local == 0) & (owner > 0)
        high = (local == 7) & (owner < elements - 1)
        here = jnp.where(low | high, 0.5, 1.0)
        there = (low & (element == owner - 1)) | (high & (element == owner + 1))
        return jnp.where(element == owner, here, jnp.where(there, 0.5, 0.0))

    pz[...] = share(
        lax.broadcasted_iota(jnp.int32, (128, lz), 1) + iz * lz,
        grid_z,
        lax.broadcasted_iota(jnp.int32, (128, lz), 0),
    )
    node = lax.broadcasted_iota(jnp.int32, (lx * ly, grid_x * grid_y), 0)
    elem = lax.broadcasted_iota(jnp.int32, (lx * ly, grid_x * grid_y), 1)
    pxy[...] = share(node // ly + ix * lx, grid_x, elem // grid_y) * share(
        node % ly + iy * ly, grid_y, elem % grid_y
    )
    here = lax.broadcasted_iota(jnp.int32, (lz, 128), 0) // 8 + iz * bz
    restr[...] = jnp.where(
        here == lax.broadcasted_iota(jnp.int32, (lz, 128), 1), wcol_ref[...] * 0.125, 0.0
    )

    gz_t, gz, gz_sq = gz_ref[0], gz_ref[1], gz_ref[2]

    def along_x(v, matrix):
        layers = [v[a * ly : (a + 1) * ly] for a in range(8)]
        out = []
        for i in range(8):
            acc = layers[0] * float(matrix[i, 0])
            for a in range(1, 8):
                acc = acc + layers[a] * float(matrix[i, a])
            out.append(acc)
        return jnp.concatenate(out, axis=0)

    def block(ref, b, lead=None):
        if lead is None:
            return ref[8 * b : 8 * b + 8].reshape(rows, lz)
        return ref[lead, 8 * b : 8 * b + 8].reshape(rows, lz)

    def assemble_block(v):
        v = (
            v
            + jnp.where(z_up, pltpu.roll(v, lz - 1, 1), 0.0)
            + jnp.where(z_down, pltpu.roll(v, 1, 1), 0.0)
        )
        return (
            v
            + jnp.where(y_up, pltpu.roll(v, rows - 1, 0), 0.0)
            + jnp.where(y_down, pltpu.roll(v, 1, 0), 0.0)
        )

    ends = (lax.broadcasted_iota(jnp.int32, (8, lz), 0) == 0) & (
        lax.broadcasted_iota(jnp.int32, (8, lz), 1) == 0
    )
    ends = ends | (
        (lax.broadcasted_iota(jnp.int32, (8, lz), 0) == 1)
        & (lax.broadcasted_iota(jnp.int32, (8, lz), 1) == lz - 1)
    )
    ends = jnp.where(ends, 1.0, 0.0).astype(F32)

    def neighbour(o):
        to = (ix + o[0], iy + o[1], iz + o[2])
        there = None
        for value, size, step in zip(to, sizes, o):
            if step:
                ok = (value >= 0) if step < 0 else (value < size)
                there = ok if there is None else (there & ok)
        return to, there

    def buffers(o, slot):
        ox, oy, oz = o
        if oz:
            out = zsend.at[slot, (oz + 1) // 2]
        elif oy:
            out = ysend.at[slot, (oy + 1) // 2]
        else:
            out = part.at[slot, 0 if ox < 0 else lx - 1]

        def land(p):
            px, py, pz_ = p
            if pz_:
                return zrecv.at[slot, (pz_ + 1) // 2, py + 1, px + 1]
            if py:
                return yrecv.at[slot, (py + 1) // 2, px + 1]
            return xrecv.at[slot, (px + 1) // 2]

        return out, land

    def exists(o):
        return all(s > 1 or not d for s, d in zip(sizes, o))

    def sending(o, slot):
        back = tuple(-d for d in o)
        out, land = buffers(o, slot)
        return pltpu.make_async_remote_copy(
            src_ref=out,
            dst_ref=land(back),
            send_sem=send_sem.at[slot, SLOT_OF[o]],
            recv_sem=recv_sem.at[slot, SLOT_OF[back]],
            device_id=neighbour(o)[0],
            device_id_type=MESH,
        )

    def receiving(o, slot):
        out, land = buffers(o, slot)
        return pltpu.make_async_remote_copy(
            src_ref=out,
            dst_ref=land(o),
            send_sem=send_sem.at[slot, SLOT_OF[o]],
            recv_sem=recv_sem.at[slot, SLOT_OF[o]],
            device_id=neighbour(o)[0],
            device_id_type=MESH,
        )

    def begin(slot, fields):
        if bx == 1:
            part[slot] = fields[0].reshape(lx, ly, lz)
        else:
            for b in range(bx):
                part[slot, 8 * b : 8 * b + 8] = fields[b].reshape(8, ly, lz)
            for b in range(bx - 1):
                both = part[slot, 8 * b + 7] + part[slot, 8 * b + 8]
                part[slot, 8 * b + 7] = both
                part[slot, 8 * b + 8] = both
        ysend[slot, 0] = part[slot, :, 0, :]
        ysend[slot, 1] = part[slot, :, ly - 1, :]
        packed = dot(ends, part[slot].reshape(lx * ly, lz), ((1,), (1,)))
        zsend[slot, 0] = packed[0:1]
        zsend[slot, 1] = packed[1:2]
        for o in OFFSETS:
            if exists(o):

                @pl.when(neighbour(o)[1])
                def _():
                    sending(o, slot).start()

    zlane = lax.broadcasted_iota(jnp.int32, (1, lx * ly), 1)

    def finish(slot):
        for o in OFFSETS:
            if exists(o):

                @pl.when(neighbour(o)[1])
                def _():
                    receiving(o, slot).wait()

        span = lx * ly
        gathered = []
        for side in range(2):
            by_y = []
            for cy in range(3):
                acc = zrecv[slot, side, cy, 1]
                if nx > 1:
                    low = pltpu.roll(zrecv[slot, side, cy, 0], ly, 1)
                    high = pltpu.roll(zrecv[slot, side, cy, 2], span - ly, 1)
                    acc = acc + jnp.where(zlane < ly, low, 0.0)
                    acc = acc + jnp.where(zlane >= span - ly, high, 0.0)
                by_y.append(acc)
            acc = by_y[1]
            acc = acc + jnp.where(zlane % ly == 0, pltpu.roll(by_y[0], span - (ly - 1), 1), 0.0)
            acc = acc + jnp.where(zlane % ly == ly - 1, pltpu.roll(by_y[2], ly - 1, 1), 0.0)
            gathered.append(acc)
        stacked = jnp.concatenate(gathered + [jnp.zeros((6, span), F32)], axis=0)
        spread = dot(stacked, ends, ((0,), (0,)))
        part[slot] = part[slot] + spread.reshape(lx, ly, lz)
        part[slot, 0] = part[slot, 0] + xrecv[slot, 0]
        part[slot, lx - 1] = part[slot, lx - 1] + xrecv[slot, 1]
        for side, at in ((0, 0), (1, ly - 1)):
            part[slot, :, at, :] = part[slot, :, at, :] + yrecv[slot, side, 1]
            part[slot, 0, at : at + 1, :] = (
                part[slot, 0, at : at + 1, :] + yrecv[slot, side, 0, lx - 1 : lx, :]
            )
            part[slot, lx - 1, at : at + 1, :] = (
                part[slot, lx - 1, at : at + 1, :] + yrecv[slot, side, 2, 0:1, :]
            )

    def gather_begin(slot):
        place[slot, me] = csend[slot]

        def send(n, carry):
            pltpu.make_async_remote_copy(
                src_ref=csend.at[slot],
                dst_ref=place.at[slot, me],
                send_sem=gsend_sem.at[slot],
                recv_sem=grecv_sem.at[slot],
                device_id=coords(lax.rem(me + n, devices)),
                device_id_type=MESH,
            ).start()
            return carry

        lax.fori_loop(1, devices, send, 0)

    def gather_finish(slot):
        most = place.at[slot, pl.ds(0, devices - 1)]
        pltpu.make_async_copy(most, most, gsend_sem.at[slot]).wait()
        pltpu.make_async_copy(most, most, grecv_sem.at[slot]).wait()
        for gx in range(nx):
            for gy in range(ny):
                tile = place[slot, (gx * ny + gy) * nz]
                for gz_ in range(1, nz):
                    tile = tile + place[slot, (gx * ny + gy) * nz + gz_]
                for ex in range(bx):
                    cgrid[gx * bx + ex, gy * by : gy * by + by, :] = tile[ex * by : ex * by + by]
        return cgrid[...]

    first = PITERS
    csend[first] = jnp.zeros((8, 128), F32)
    for ex in range(bx):
        csend[first, ex * by : ex * by + by, 0:bz] = off_ref[ex]
    shift = jnp.where(
        lax.broadcasted_iota(jnp.int32, (128, 128), 0) + iz * bz
        == lax.broadcasted_iota(jnp.int32, (128, 128), 1),
        1.0,
        0.0,
    ).astype(F32)
    keep = lax.broadcasted_iota(jnp.int32, (8, 128), 1) < bz
    csend[first] = dot(jnp.where(keep, csend[first], 0.0), shift)

    fields = []
    for b in range(bx):
        t = block(temp_ref, b)
        w = block(weight, b)
        wk = w * block(cond_ref, b)
        tx, ty, tz = along_x(t, derivs), dot(ky_ref[0], t), dot(t, gz_t)
        advect = block(flow_ref, b, 0) * tx + block(flow_ref, b, 1) * ty
        advect = advect + block(flow_ref, b, 2) * tz
        diffuse = along_x(wk * tx, derivs.T) + dot(ky_ref[1], wk * ty) + dot(wk * tz, gz)
        fields.append(assemble_block(-(w * advect) - diffuse))

    pl.semaphore_wait(barrier, devices - 1)
    begin(0, fields)
    gather_begin(first)
    fields = []
    squares = (derivs * derivs).T
    for b in range(bx):
        c = block(coef, b)
        jac = along_x(c, squares) + dot(ky_ref[2], c) + dot(c, gz_sq) + HELM_SHIFT * block(weight, b)
        fields.append(assemble_block(jac))
    begin(1, fields)

    def half_if(node_id, count):
        local = node_id % 8
        shared = ((local == 0) & (node_id > 0)) | ((local == 7) & (node_id < count - 1))
        return jnp.where(shared, 0.5, 1.0)

    yz_share = half_if(lax.broadcasted_iota(jnp.int32, (ly, lz), 0) + iy * ly, ny * ly)
    yz_share = yz_share * half_if(lax.broadcasted_iota(jnp.int32, (ly, lz), 1) + iz * lz, nz * lz)
    yz_share = yz_share / wyz_ref[...] * CLOCK_STEP_SIZE

    finish(0)
    for x in range(lx):
        x_share = half_if(jnp.full((ly, lz), x, jnp.int32) + ix * lx, nx * lx)
        scale = yz_share * (x_share * float(1.0 / weights[x % 8]))
        newt_ref[x] = temp_ref[x] + part[0, x] * scale

    fields = []
    for b in range(bx):
        w = block(weight, b)
        out = along_x(w * block(flow_ref, b, 0), derivs.T)
        out = out + dot(ky_ref[1], w * block(flow_ref, b, 1))
        out = out + dot(w * (block(flow_ref, b, 2) + block(newt_ref, b)), gz)
        fields.append(assemble_block(out))
    begin(2, fields)
    finish(1)
    q[...] = 1.0 / part[1]
    shift_c = 6.0 + gather_finish(first)
    padded[...] = jnp.zeros(padded.shape, F32)
    finish(2)
    resid_ref[...] = part[2]
    start, steps = fine_coefficients()
    direc[...] = resid_ref[...] * q[...] * start
    press_ref[...] = direc[...]

    cs = (grid_x, grid_y, 128)
    cinv = 1.0 / shift_c
    cl = lax.broadcasted_iota(jnp.int32, cs, 2)
    c_up = cl < grid_z - 1
    c_down = (cl > 0) & (cl < grid_z)

    def coarse_apply(v):
        padded[1 : grid_x + 1, 8 : 8 + grid_y, :] = v
        beside = padded[0:grid_x, 8 : 8 + grid_y, :] + padded[2 : grid_x + 2, 8 : 8 + grid_y, :]
        beside = beside + padded[1 : grid_x + 1, 7 : 7 + grid_y, :]
        beside = beside + padded[1 : grid_x + 1, 9 : 9 + grid_y, :]
        beside = beside + jnp.where(c_up, pltpu.roll(v, 127, 2), 0.0)
        beside = beside + jnp.where(c_down, pltpu.roll(v, 1, 2), 0.0)
        return shift_c * v - beside

    def coarse_solve(r):
        centre = 0.5 * (COARSE_HIGH + COARSE_LOW)
        half = 0.5 * (COARSE_HIGH - COARSE_LOW)
        ratio = centre / half
        rho = 1.0 / ratio
        d = r * cinv * (1.0 / centre)
        sol = d
        for _ in range(1, CHEB_C):
            r = r - coarse_apply(d)
            new = 1.0 / (2.0 * ratio - rho)
            d = (new * rho) * d + (2.0 * new / half) * (r * cinv)
            sol = sol + d
            rho = new
        return sol

    cycle = SMOOTH + 1
    total = PITERS * cycle

    def step(t, carry):
        k = lax.rem(t, cycle)
        slot = lax.rem(t, 2)
        made = []
        for b in range(bx):
            v = block(direc, b)
            c = block(coef, b)
            out = along_x(c * along_x(v, derivs), derivs.T)
            out = out + dot(ky_ref[1], c * dot(ky_ref[0], v))
            out = out + dot(c * dot(v, gz_t), gz)
            made.append(assemble_block(out + HELM_SHIFT * block(weight, b) * v))
        begin(slot, made)
        finish(slot)
        resid_ref[...] = resid_ref[...] - part[slot]

        @pl.when(k == SMOOTH - 1)
        def _():
            turn = lax.div(t, cycle)
            csend[turn] = dot(
                dot(wrow_ref[...], resid_ref[...].reshape(lx * ly, lz)), restr[...]
            )
            gather_begin(turn)
            sol = coarse_solve(gather_finish(turn))
            spread = dot(sol.reshape(grid_x * grid_y, 128), pz[...])
            direc[...] = dot(pxy[...], spread).reshape(lx, ly, lz)

        @pl.when(k != SMOOTH - 1)
        def _():
            alpha = jnp.float32(0.0)
            beta = jnp.float32(start)
            for n, (a, b) in enumerate(steps):
                alpha = jnp.where(k == n, jnp.float32(a), alpha)
                beta = jnp.where(k == n, jnp.float32(b), beta)
            direc[...] = alpha * direc[...] + beta * (resid_ref[...] * q[...])

        @pl.when(t < total - 1)
        def _():
            press_ref[...] = press_ref[...] + direc[...]

        return carry

    lax.fori_loop(0, total, step, 0)


def shards(sizes, temp, flow, cond, vol, off):
    derivs, weights = gll_tables()
    lx, ly, lz = temp.shape
    blocks = off.shape
    bx, by, bz = blocks
    devices = sizes[0] * sizes[1] * sizes[2]
    squares = derivs * derivs
    eye_z = np.eye(bz, dtype=np.float32)
    eye_y = np.eye(ly, dtype=np.float32)
    gz = np.stack([np.kron(eye_z, derivs.T), np.kron(eye_z, derivs), np.kron(eye_z, squares)])
    ky = np.stack([np.kron(eye_y, derivs), np.kron(eye_y, derivs.T), np.kron(eye_y, squares.T)])
    w_y, w_z = np.tile(weights, by), np.tile(weights, bz)
    wyz = w_y[:, None] * w_z[None, :]
    wcol = np.broadcast_to(w_z[:, None], (lz, 128))
    wrow = np.zeros((8, lx * ly), np.float32)
    for ex in range(bx):
        for ey in range(by):
            for a in range(8):
                at = (ex * 8 + a) * ly + ey * 8
                wrow[ex * by + ey, at : at + 8] = weights[a] * weights
    cube = jax.ShapeDtypeStruct((lx, ly, lz), jnp.float32)
    vmem = pl.BlockSpec(memory_space=pltpu.VMEM)
    grid = (sizes[0] * bx, sizes[1] * by)
    scratch = [
        pltpu.VMEM((lx, ly, lz), F32),
        pltpu.VMEM((lx, ly, lz), F32),
        pltpu.VMEM((lx, ly, lz), F32),
        pltpu.VMEM((lx, ly, lz), F32),
        pltpu.VMEM((3, lx, ly, lz), F32),
        pltpu.VMEM((3, 2, lx, lz), F32),
        pltpu.VMEM((3, 2, 1, lx * ly), F32),
        pltpu.VMEM((3, 2, ly, lz), F32),
        pltpu.VMEM((3, 2, 3, lx, lz), F32),
        pltpu.VMEM((3, 2, 3, 3, 1, lx * ly), F32),
        pltpu.VMEM((PITERS + 1, devices, 8, 128), F32),
        pltpu.VMEM((PITERS + 1, 8, 128), F32),
        pltpu.VMEM((grid[0], grid[1], 128), F32),
        pltpu.VMEM((grid[0] + 2, grid[1] + 16, 128), F32),
        pltpu.VMEM((128, lz), F32),
        pltpu.VMEM((lx * ly, grid[0] * grid[1]), F32),
        pltpu.VMEM((lz, 128), F32),
        pltpu.SemaphoreType.DMA((3, len(OFFSETS))),
        pltpu.SemaphoreType.DMA((3, len(OFFSETS))),
        pltpu.SemaphoreType.DMA((PITERS + 1,)),
        pltpu.SemaphoreType.DMA((PITERS + 1,)),
    ]
    return pl.pallas_call(
        functools.partial(kernel, sizes, blocks),
        out_shape=(cube, cube, cube),
        in_specs=[vmem] * 10,
        out_specs=(vmem, vmem, vmem),
        scratch_shapes=scratch,
        compiler_params=pltpu.CompilerParams(
            collective_id=0, has_side_effects=True, vmem_limit_bytes=40 * 1024 * 1024
        ),
        name="spectral_step",
    )(temp, flow, cond, vol, off, gz, ky, wyz, wcol, wrow)


def solution(mesh):
    cube = P("gx", "gy", "gz")
    sizes = tuple(mesh.shape[name] for name in ("gx", "gy", "gz"))
    return jax.shard_map(
        functools.partial(shards, sizes),
        mesh=mesh,
        in_specs=(cube, P(None, "gx", "gy", "gz"), cube, cube, cube),
        out_specs=(cube, cube, cube),
        check_vma=False,
    )
```

```python
import functools
import itertools

import jax
import jax.numpy as jnp
import numpy as np
from jax import lax
from jax.experimental import pallas as pl
from jax.experimental.pallas import tpu as pltpu
from jax.sharding import PartitionSpec as P

PITERS = 2
SMOOTH = 3
CHEB_C = 8
CLOCK_STEP_SIZE = 0.0002
HELM_SHIFT = 1.0
FINE_LOW = 0.25
FINE_HIGH = 3.0
COARSE_LOW = 0.07
COARSE_HIGH = 2.0
GLL_POINTS = (
    -1.0,
    -0.8717401485096066,
    -0.5917001814331423,
    -0.2092992179024789,
    0.2092992179024789,
    0.5917001814331423,
    0.8717401485096066,
    1.0,
)
MESH = pl.DeviceIdType.MESH
HIGHEST = lax.Precision.HIGHEST
F32 = jnp.float32
OFFSETS = [o for o in itertools.product((-1, 0, 1), repeat=3) if o != (0, 0, 0)]
SLOT_OF = {o: n for n, o in enumerate(OFFSETS)}


def legendre_seven(point):
    p_prev = 1.0
    p_cur = point
    for order_k in range(1, 7):
        p_next = ((2.0 * order_k + 1.0) * point * p_cur - order_k * p_prev) / (order_k + 1.0)
        p_prev = p_cur
        p_cur = p_next
    return p_cur


def gll_tables():
    points = GLL_POINTS
    legend = [legendre_seven(point) for point in points]
    weights = [2.0 / (56.0 * value * value) for value in legend]
    derivs = np.zeros((8, 8))
    for i in range(8):
        for a in range(8):
            if i != a:
                derivs[i, a] = legend[i] / (legend[a] * (points[i] - points[a]))
    derivs[0, 0] = -14.0
    derivs[7, 7] = 14.0
    return derivs.astype(np.float32), np.asarray(weights, np.float32)


def dot(a, b, dims=((1,), (0,))):
    return lax.dot_general(a, b, (dims, ((), ())), precision=HIGHEST, preferred_element_type=F32)


BF16 = jnp.bfloat16


def narrow(v, terms):
    out = []
    for n in range(terms):
        piece = v.astype(BF16)
        out.append(piece)
        if n < terms - 1:
            v = v - piece.astype(F32)
    return out


def bdot(a, b, dims=((1,), (0,))):
    return lax.dot_general(a, b, (dims, ((), ())), preferred_element_type=F32)


def right(v, pair):
    width = v.shape[1]
    out = bdot(jnp.concatenate(narrow(v, 2), axis=1), pair)
    return out[:, :width] + out[:, width:]


def left(high, low, v):
    width = v.shape[1]
    pieces = narrow(v, 2)
    out = bdot(high, jnp.concatenate(pieces, axis=1))
    return out[:, :width] + out[:, width:] + bdot(low, pieces[0])


def reach(sizes, blocks):
    out = []
    for o in itertools.product(*(range(1 - s, s) for s in sizes)):
        far = sum(max(abs(d) - 1, 0) * b for d, b in zip(o, blocks))
        if far < CHEB_C and o != (0, 0, 0):
            out.append(o)
    return out


def fine_coefficients():
    centre = 0.5 * (FINE_HIGH + FINE_LOW)
    half = 0.5 * (FINE_HIGH - FINE_LOW)
    ratio = centre / half
    rho = 1.0 / ratio
    steps = []
    for _ in range(1, SMOOTH):
        new = 1.0 / (2.0 * ratio - rho)
        steps.append((new * rho, 2.0 * new / half))
        rho = new
    return 1.0 / centre, steps


def kernel(
    sizes,
    blocks,
    temp_hbm,
    flow_hbm,
    cond_hbm,
    vol_hbm,
    off_ref,
    mats_ref,
    rows_ref,
    newt_ref,
    press_ref,
    resid_ref,
    temp_ref,
    flow_ref,
    cond_ref,
    vol_ref,
    in_sem,
    weight,
    coef,
    q,
    direc,
    part,
    ysend,
    zsend,
    xrecv,
    yrecv,
    zrecv,
    place,
    csend,
    ctile,
    cgrid,
    padded,
    pz,
    pxy,
    send_sem,
    recv_sem,
    gsend_sem,
    grecv_sem,
):
    derivs, weights = gll_tables()
    nx, ny, nz = sizes
    bx, by, bz = blocks
    lx, ly, lz = 8 * bx, 8 * by, 8 * bz
    rows = 8 * ly
    devices = nx * ny * nz
    grid_x, grid_y, grid_z = nx * bx, ny * by, nz * bz
    ix, iy, iz = lax.axis_index("gx"), lax.axis_index("gy"), lax.axis_index("gz")
    me = (ix * ny + iy) * nz + iz

    loads = [
        pltpu.make_async_copy(a, b, in_sem.at[n])
        for n, (a, b) in enumerate(
            (
                (temp_hbm, temp_ref),
                (flow_hbm, flow_ref),
                (cond_hbm, cond_ref),
                (vol_hbm, vol_ref),
            )
        )
    ]
    for load in loads:
        load.start()

    xrecv[...] = jnp.zeros(xrecv.shape, F32)
    yrecv[...] = jnp.zeros(yrecv.shape, F32)
    zrecv[...] = jnp.zeros(zrecv.shape, F32)
    place[...] = jnp.zeros(place.shape, F32)
    partners = reach(sizes, blocks)

    def neighbour(o):
        to = (ix + o[0], iy + o[1], iz + o[2])
        there = None
        for value, size, step in zip(to, sizes, o):
            if step:
                ok = (value >= 0) if step < 0 else (value < size)
                there = ok if there is None else (there & ok)
        return to, there

    barrier = pltpu.get_barrier_semaphore()

    met = jnp.int32(0)
    for o in partners:
        to, there = neighbour(o)
        met = met + jnp.where(there, 1, 0)

        @pl.when(there)
        def _():
            pl.semaphore_signal(barrier, inc=1, device_id=to, device_id_type=MESH)

    lane = lax.broadcasted_iota(jnp.int32, (rows, lz), 1)
    row_y = lax.broadcasted_iota(jnp.int32, (rows, lz), 0) % ly
    z_up = (lane % 8 == 7) & (lane < lz - 1)
    z_down = (lane % 8 == 0) & (lane > 0)
    y_up = (row_y % 8 == 7) & (row_y < ly - 1)
    y_down = (row_y % 8 == 0) & (row_y > 0)

    wyz = rows_ref[0:ly]
    for x in range(lx):
        weight[x] = wyz * float(weights[x % 8])

    def share(node, elements, element):
        owner = node // 8
        local = node % 8
        low = (local == 0) & (owner > 0)
        high = (local == 7) & (owner < elements - 1)
        here = jnp.where(low | high, 0.5, 1.0)
        there = (low & (element == owner - 1)) | (high & (element == owner + 1))
        return jnp.where(element == owner, here, jnp.where(there, 0.5, 0.0))

    pz[...] = share(
        lax.broadcasted_iota(jnp.int32, (128, lz), 1) + iz * lz,
        grid_z,
        lax.broadcasted_iota(jnp.int32, (128, lz), 0),
    ).astype(BF16)
    node = lax.broadcasted_iota(jnp.int32, (lx * ly, grid_x * grid_y), 0)
    elem = lax.broadcasted_iota(jnp.int32, (lx * ly, grid_x * grid_y), 1)
    pxy[...] = (
        share(node // ly + ix * lx, grid_x, elem // grid_y)
        * share(node % ly + iy * ly, grid_y, elem % grid_y)
    ).astype(BF16)
    restr = rows_ref[ly : ly + 128]
    spot = lax.broadcasted_iota(jnp.int32, (8, 128), 1)
    own_row = spot // bz == lax.broadcasted_iota(jnp.int32, (8, 128), 0)
    from_lane = lax.broadcasted_iota(jnp.int32, (128, 128), 0)
    to_lane = lax.broadcasted_iota(jnp.int32, (128, 128), 1)
    fold = jnp.where(from_lane % bz == to_lane % bz, 1.0, 0.0).astype(BF16)

    def along_z(v, n):
        return right(v, mats_ref[n])

    def along_y(v, n):
        return left(mats_ref[3 + n], mats_ref[6 + n], v)

    def along_x(v, matrix):
        layers = [v[a * ly : (a + 1) * ly] for a in range(8)]
        out = []
        for i in range(8):
            acc = layers[0] * float(matrix[i, 0])
            for a in range(1, 8):
                acc = acc + layers[a] * float(matrix[i, a])
            out.append(acc)
        return jnp.concatenate(out, axis=0)

    def block(ref, b, lead=None):
        if lead is None:
            return ref[8 * b : 8 * b + 8].reshape(rows, lz)
        return ref[lead, 8 * b : 8 * b + 8].reshape(rows, lz)

    def assemble_block(v):
        v = (
            v
            + jnp.where(z_up, pltpu.roll(v, lz - 1, 1), 0.0)
            + jnp.where(z_down, pltpu.roll(v, 1, 1), 0.0)
        )
        return (
            v
            + jnp.where(y_up, pltpu.roll(v, rows - 1, 0), 0.0)
            + jnp.where(y_down, pltpu.roll(v, 1, 0), 0.0)
        )

    end_row = lax.broadcasted_iota(jnp.int32, (16, lz), 0)
    end_lane = lax.broadcasted_iota(jnp.int32, (16, lz), 1)
    ends = jnp.where(
        (end_row < 6) & (end_lane == jnp.where(end_row % 2 == 0, 0, lz - 1)), 1.0, 0.0
    ).astype(BF16)
    ends_three = jnp.concatenate([ends] * 3, axis=1)

    def buffers(o, slot):
        ox, oy, oz = o
        if oz:
            out = zsend.at[slot, (oz + 1) // 2]
        elif oy:
            out = ysend.at[slot, (oy + 1) // 2]
        else:
            out = part.at[slot, 0 if ox < 0 else lx - 1]

        def land(p):
            px, py, pz_ = p
            if pz_:
                return zrecv.at[slot, (pz_ + 1) // 2, py + 1, px + 1]
            if py:
                return yrecv.at[slot, (py + 1) // 2, px + 1]
            return xrecv.at[slot, (px + 1) // 2]

        return out, land

    def exists(o):
        return all(s > 1 or not d for s, d in zip(sizes, o))

    def sending(o, slot):
        back = tuple(-d for d in o)
        out, land = buffers(o, slot)
        return pltpu.make_async_remote_copy(
            src_ref=out,
            dst_ref=land(back),
            send_sem=send_sem.at[slot, SLOT_OF[o]],
            recv_sem=recv_sem.at[slot, SLOT_OF[back]],
            device_id=neighbour(o)[0],
            device_id_type=MESH,
        )

    def receiving(o, slot):
        out, land = buffers(o, slot)
        return pltpu.make_async_remote_copy(
            src_ref=out,
            dst_ref=land(o),
            send_sem=send_sem.at[slot, SLOT_OF[o]],
            recv_sem=recv_sem.at[slot, SLOT_OF[o]],
            device_id=neighbour(o)[0],
            device_id_type=MESH,
        )

    def begin(slot, fields):
        if bx == 1:
            part[slot] = fields[0].reshape(lx, ly, lz)
        else:
            for b in range(bx):
                part[slot, 8 * b : 8 * b + 8] = fields[b].reshape(8, ly, lz)
            for b in range(bx - 1):
                both = part[slot, 8 * b + 7] + part[slot, 8 * b + 8]
                part[slot, 8 * b + 7] = both
                part[slot, 8 * b + 8] = both
        ysend[slot, 0] = part[slot, :, 0, :]
        ysend[slot, 1] = part[slot, :, ly - 1, :]
        whole = jnp.concatenate(narrow(part[slot].reshape(lx * ly, lz), 3), axis=1)
        packed = bdot(ends_three, whole, ((1,), (1,)))
        zsend[slot, 0] = packed[0:1]
        zsend[slot, 1] = packed[1:2]
        for o in OFFSETS:
            if exists(o):

                @pl.when(neighbour(o)[1])
                def _():
                    sending(o, slot).start()

    zlane = lax.broadcasted_iota(jnp.int32, (1, lx * ly), 1)

    def finish(slot):
        for o in OFFSETS:
            if exists(o):

                @pl.when(neighbour(o)[1])
                def _():
                    receiving(o, slot).wait()

        span = lx * ly
        gathered = []
        for side in range(2):
            by_y = []
            for cy in range(3):
                acc = zrecv[slot, side, cy, 1]
                if nx > 1:
                    low = pltpu.roll(zrecv[slot, side, cy, 0], ly, 1)
                    high = pltpu.roll(zrecv[slot, side, cy, 2], span - ly, 1)
                    acc = acc + jnp.where(zlane < ly, low, 0.0)
                    acc = acc + jnp.where(zlane >= span - ly, high, 0.0)
                by_y.append(acc)
            acc = by_y[1]
            acc = acc + jnp.where(zlane % ly == 0, pltpu.roll(by_y[0], span - (ly - 1), 1), 0.0)
            acc = acc + jnp.where(zlane % ly == ly - 1, pltpu.roll(by_y[2], ly - 1, 1), 0.0)
            gathered.append(acc)
        pieces = [p.astype(F32) for p in narrow(jnp.concatenate(gathered, axis=0), 3)]
        stacked = jnp.concatenate(pieces + [jnp.zeros((10, span), F32)], axis=0)
        spread = bdot(stacked.astype(BF16), ends, ((0,), (0,)))
        part[slot] = part[slot] + spread.reshape(lx, ly, lz)
        part[slot, 0] = part[slot, 0] + xrecv[slot, 0]
        part[slot, lx - 1] = part[slot, lx - 1] + xrecv[slot, 1]
        for side, at in ((0, 0), (1, ly - 1)):
            part[slot, :, at, :] = part[slot, :, at, :] + yrecv[slot, side, 1]
            part[slot, 0, at : at + 1, :] = (
                part[slot, 0, at : at + 1, :] + yrecv[slot, side, 0, lx - 1 : lx, :]
            )
            part[slot, lx - 1, at : at + 1, :] = (
                part[slot, lx - 1, at : at + 1, :] + yrecv[slot, side, 2, 0:1, :]
            )

    def gather_begin(slot, tile):
        csend[slot] = jnp.sum(jnp.where(own_row, tile, 0.0), axis=0, keepdims=True)
        place[slot, me] = csend[slot]
        for o in partners:
            to, there = neighbour(o)

            @pl.when(there)
            def _():
                gather_copy(slot, o).start()

    def gather_copy(slot, o, arriving=False):
        to, _ = neighbour(o)
        other = (to[0] * ny + to[1]) * nz + to[2]
        return pltpu.make_async_remote_copy(
            src_ref=csend.at[slot],
            dst_ref=place.at[slot, other if arriving else me],
            send_sem=gsend_sem.at[slot, partners.index(o)],
            recv_sem=grecv_sem.at[slot, partners.index(tuple(d if arriving else -d for d in o))],
            device_id=to,
            device_id_type=MESH,
        )

    def gather_finish(slot):
        for o in partners:
            to, there = neighbour(o)

            @pl.when(there)
            def _():
                gather_copy(slot, o, True).wait()

        shape = (devices, 8, 128)
        box_lane = lax.broadcasted_iota(jnp.int32, shape, 2) // bz
        box_row = lax.broadcasted_iota(jnp.int32, shape, 1)
        box_z = lax.broadcasted_iota(jnp.int32, shape, 0) % nz
        boxes = jnp.where(box_lane == box_row, jnp.broadcast_to(place[slot], shape), 0.0)
        boxes = boxes.reshape(devices * 8, 128)
        moved = bdot(jnp.concatenate(narrow(boxes, 3), axis=1), jnp.concatenate([fold] * 3, axis=0))
        moved = jnp.where(box_lane == box_z, moved.reshape(shape), 0.0)
        for gx in range(nx):
            for gy in range(ny):
                at = (gx * ny + gy) * nz
                tile = moved[at]
                for gz in range(1, nz):
                    tile = tile + moved[at + gz]
                for ex in range(bx):
                    cgrid[gx * bx + ex, gy * by : gy * by + by, :] = tile[ex * by : ex * by + by]
        return cgrid[...]

    first = PITERS
    ctile[...] = jnp.zeros((8, 128), F32)
    for ex in range(bx):
        ctile[ex * by : ex * by + by, 0:bz] = off_ref[ex]
    spread_out = jnp.where((from_lane < bz) & (from_lane == to_lane % bz), 1.0, 0.0).astype(F32)
    off_tile = dot(ctile[...], spread_out)
    for load in loads:
        load.wait()
    coef[...] = weight[...] * vol_ref[...]

    fields = []
    for b in range(bx):
        t = block(temp_ref, b)
        w = block(weight, b)
        wk = w * block(cond_ref, b)
        tx, ty, tz = along_x(t, derivs), along_y(t, 0), along_z(t, 0)
        advect = block(flow_ref, b, 0) * tx + block(flow_ref, b, 1) * ty
        advect = advect + block(flow_ref, b, 2) * tz
        diffuse = along_x(wk * tx, derivs.T) + along_y(wk * ty, 1) + along_z(wk * tz, 1)
        fields.append(assemble_block(-(w * advect) - diffuse))

    pl.semaphore_wait(barrier, met)
    begin(0, fields)
    gather_begin(first, off_tile)
    fields = []
    squares = (derivs * derivs).T
    for b in range(bx):
        c = block(coef, b)
        jac = along_x(c, squares) + along_y(c, 2) + along_z(c, 2) + HELM_SHIFT * block(weight, b)
        fields.append(assemble_block(jac))
    begin(1, fields)

    def half_if(node_id, count):
        local = node_id % 8
        shared = ((local == 0) & (node_id > 0)) | ((local == 7) & (node_id < count - 1))
        return jnp.where(shared, 0.5, 1.0)

    yz_share = half_if(lax.broadcasted_iota(jnp.int32, (ly, lz), 0) + iy * ly, ny * ly)
    yz_share = yz_share * half_if(lax.broadcasted_iota(jnp.int32, (ly, lz), 1) + iz * lz, nz * lz)
    yz_share = yz_share / wyz * CLOCK_STEP_SIZE

    finish(0)
    for x in range(lx):
        x_share = half_if(jnp.full((ly, lz), x, jnp.int32) + ix * lx, nx * lx)
        scale = yz_share * (x_share * float(1.0 / weights[x % 8]))
        newt_ref[x] = temp_ref[x] + part[0, x] * scale

    fields = []
    for b in range(bx):
        w = block(weight, b)
        out = along_x(w * block(flow_ref, b, 0), derivs.T)
        out = out + along_y(w * block(flow_ref, b, 1), 1)
        out = out + along_z(w * (block(flow_ref, b, 2) + block(newt_ref, b)), 1)
        fields.append(assemble_block(out))
    begin(2, fields)
    finish(1)
    q[...] = 1.0 / part[1]
    shift_c = 6.0 + gather_finish(first)
    padded[...] = jnp.zeros(padded.shape, F32)
    finish(2)
    resid_ref[...] = part[2]
    start, steps = fine_coefficients()
    direc[...] = resid_ref[...] * q[...] * start
    press_ref[...] = direc[...]

    cs = (grid_x, grid_y, 128)
    cinv = 1.0 / shift_c
    cl = lax.broadcasted_iota(jnp.int32, cs, 2)
    c_up = cl < grid_z - 1
    c_down = (cl > 0) & (cl < grid_z)

    def coarse_apply(v):
        padded[1 : grid_x + 1, 8 : 8 + grid_y, :] = v
        beside = padded[0:grid_x, 8 : 8 + grid_y, :] + padded[2 : grid_x + 2, 8 : 8 + grid_y, :]
        beside = beside + padded[1 : grid_x + 1, 7 : 7 + grid_y, :]
        beside = beside + padded[1 : grid_x + 1, 9 : 9 + grid_y, :]
        beside = beside + jnp.where(c_up, pltpu.roll(v, 127, 2), 0.0)
        beside = beside + jnp.where(c_down, pltpu.roll(v, 1, 2), 0.0)
        return shift_c * v - beside

    def coarse_solve(r):
        centre = 0.5 * (COARSE_HIGH + COARSE_LOW)
        half = 0.5 * (COARSE_HIGH - COARSE_LOW)
        ratio = centre / half
        rho = 1.0 / ratio
        d = r * cinv * (1.0 / centre)
        sol = d
        for _ in range(1, CHEB_C):
            r = r - coarse_apply(d)
            new = 1.0 / (2.0 * ratio - rho)
            d = (new * rho) * d + (2.0 * new / half) * (r * cinv)
            sol = sol + d
            rho = new
        return sol

    cycle = SMOOTH + 1
    total = PITERS * cycle

    def step(t, carry):
        k = lax.rem(t, cycle)
        slot = lax.rem(t, 2)
        made = []
        for b in range(bx):
            v = block(direc, b)
            c = block(coef, b)
            out = along_x(c * along_x(v, derivs), derivs.T)
            out = out + along_y(c * along_y(v, 0), 1)
            out = out + along_z(c * along_z(v, 0), 1)
            made.append(assemble_block(out + HELM_SHIFT * block(weight, b) * v))
        begin(slot, made)
        finish(slot)
        resid_ref[...] = resid_ref[...] - part[slot]

        @pl.when(k == SMOOTH - 1)
        def _():
            turn = lax.div(t, cycle)
            sums = []
            for b in range(bx):
                acc = resid_ref[8 * b] * float(weights[0])
                for a in range(1, 8):
                    acc = acc + resid_ref[8 * b + a] * float(weights[a])
                sums.append(acc * rows_ref[ly + 128 : 2 * ly + 128])
            sums = dot(jnp.concatenate(sums, axis=0), restr)
            gather_begin(turn, jnp.sum(sums.reshape(bx * by, 8, 128), axis=1))
            sol = coarse_solve(gather_finish(turn)).reshape(grid_x * grid_y, 128)
            count = grid_x * grid_y
            along = bdot(jnp.concatenate(narrow(sol, 3), axis=0), pz[...])
            along = along[0:count] + along[count : 2 * count] + along[2 * count :]
            wide = bdot(pxy[...], jnp.concatenate(narrow(along, 3), axis=1))
            wide = wide[:, 0:lz] + wide[:, lz : 2 * lz] + wide[:, 2 * lz :]
            direc[...] = wide.reshape(lx, ly, lz)

        @pl.when(k != SMOOTH - 1)
        def _():
            alpha = jnp.float32(0.0)
            beta = jnp.float32(start)
            for n, (a, b) in enumerate(steps):
                alpha = jnp.where(k == n, jnp.float32(a), alpha)
                beta = jnp.where(k == n, jnp.float32(b), beta)
            direc[...] = alpha * direc[...] + beta * (resid_ref[...] * q[...])

        @pl.when(t < total - 1)
        def _():
            press_ref[...] = press_ref[...] + direc[...]

        return carry

    lax.fori_loop(0, total, step, 0)


def shards(sizes, temp, flow, cond, vol, off):
    derivs, weights = gll_tables()
    lx, ly, lz = temp.shape
    blocks = off.shape
    bx, by, bz = blocks
    devices = sizes[0] * sizes[1] * sizes[2]
    squares = derivs * derivs
    eye_z = np.eye(bz, dtype=np.float32)
    eye_y = np.eye(ly, dtype=np.float32)

    def halves(m):
        high = m.astype(BF16)
        return high, (m - high.astype(np.float32)).astype(BF16)

    mats = np.zeros((9, 8 * ly, 8 * ly), BF16)
    for n, m in enumerate((derivs.T, derivs, squares)):
        high, low = halves(np.kron(eye_z, m))
        mats[n, :lz, :lz] = high
        mats[n, :lz, lz:] = low
        mats[n, lz:, :lz] = high
        mats[3 + n], mats[6 + n] = halves(np.kron(eye_y, m.T))
    w_y, w_z = np.tile(weights, by), np.tile(weights, bz)
    wyz = w_y[:, None] * w_z[None, :]
    lanes = np.arange(128)[None, :] % bz == np.arange(lz)[:, None] // 8
    restr = np.where(lanes, w_z[:, None] * np.float32(0.125), np.float32(0.0))
    wy_rows = np.broadcast_to(w_y[:, None], (ly, 128))
    table = np.concatenate([wyz, restr, wy_rows], axis=0).astype(np.float32)
    cube = jax.ShapeDtypeStruct((lx, ly, lz), jnp.float32)
    vmem = pl.BlockSpec(memory_space=pltpu.VMEM)
    grid = (sizes[0] * bx, sizes[1] * by)
    hbm = pl.BlockSpec(memory_space=pl.ANY)
    span = len(reach(sizes, blocks))
    scratch = [
        pltpu.VMEM((lx, ly, lz), F32),
        pltpu.VMEM((3, lx, ly, lz), F32),
        pltpu.VMEM((lx, ly, lz), F32),
        pltpu.VMEM((lx, ly, lz), F32),
        pltpu.SemaphoreType.DMA((4,)),
        pltpu.VMEM((lx, ly, lz), F32),
        pltpu.VMEM((lx, ly, lz), F32),
        pltpu.VMEM((lx, ly, lz), F32),
        pltpu.VMEM((lx, ly, lz), F32),
        pltpu.VMEM((3, lx, ly, lz), F32),
        pltpu.VMEM((3, 2, lx, lz), F32),
        pltpu.VMEM((3, 2, 1, lx * ly), F32),
        pltpu.VMEM((3, 2, ly, lz), F32),
        pltpu.VMEM((3, 2, 3, lx, lz), F32),
        pltpu.VMEM((3, 2, 3, 3, 1, lx * ly), F32),
        pltpu.VMEM((PITERS + 1, devices, 1, 128), F32),
        pltpu.VMEM((PITERS + 1, 1, 128), F32),
        pltpu.VMEM((8, 128), F32),
        pltpu.VMEM((grid[0], grid[1], 128), F32),
        pltpu.VMEM((grid[0] + 2, grid[1] + 16, 128), F32),
        pltpu.VMEM((128, lz), BF16),
        pltpu.VMEM((lx * ly, grid[0] * grid[1]), BF16),
        pltpu.SemaphoreType.DMA((3, len(OFFSETS))),
        pltpu.SemaphoreType.DMA((3, len(OFFSETS))),
        pltpu.SemaphoreType.DMA((PITERS + 1, span)),
        pltpu.SemaphoreType.DMA((PITERS + 1, span)),
    ]
    return pl.pallas_call(
        functools.partial(kernel, sizes, blocks),
        out_shape=(cube, cube, cube),
        in_specs=[hbm] * 4 + [vmem] * 3,
        out_specs=(vmem, vmem, vmem),
        scratch_shapes=scratch,
        compiler_params=pltpu.CompilerParams(
            collective_id=0, has_side_effects=True, vmem_limit_bytes=40 * 1024 * 1024
        ),
        name="spectral_step",
    )(temp, flow, cond, vol, off, jnp.asarray(mats), jnp.asarray(table))


def solution(mesh):
    cube = P("gx", "gy", "gz")
    sizes = tuple(mesh.shape[name] for name in ("gx", "gy", "gz"))
    return jax.shard_map(
        functools.partial(shards, sizes),
        mesh=mesh,
        in_specs=(cube, P(None, "gx", "gy", "gz"), cube, cube, cube),
        out_specs=(cube, cube, cube),
        check_vma=False,
    )
```

```python
import functools
import itertools

import jax
import jax.numpy as jnp
import numpy as np
from jax import lax
from jax.experimental import pallas as pl
from jax.experimental.pallas import tpu as pltpu
from jax.sharding import PartitionSpec as P

PITERS = 2
SMOOTH = 3
CHEB_C = 8
CLOCK_STEP_SIZE = 0.0002
HELM_SHIFT = 1.0
FINE_LOW = 0.25
FINE_HIGH = 3.0
COARSE_LOW = 0.07
COARSE_HIGH = 2.0
GLL_POINTS = (
    -1.0,
    -0.8717401485096066,
    -0.5917001814331423,
    -0.2092992179024789,
    0.2092992179024789,
    0.5917001814331423,
    0.8717401485096066,
    1.0,
)
MESH = pl.DeviceIdType.MESH
HIGHEST = lax.Precision.HIGHEST
F32 = jnp.float32
OFFSETS = [o for o in itertools.product((-1, 0, 1), repeat=3) if o != (0, 0, 0)]
SLOT_OF = {o: n for n, o in enumerate(OFFSETS)}


def legendre_seven(point):
    p_prev = 1.0
    p_cur = point
    for order_k in range(1, 7):
        p_next = ((2.0 * order_k + 1.0) * point * p_cur - order_k * p_prev) / (order_k + 1.0)
        p_prev = p_cur
        p_cur = p_next
    return p_cur


def gll_tables():
    points = GLL_POINTS
    legend = [legendre_seven(point) for point in points]
    weights = [2.0 / (56.0 * value * value) for value in legend]
    derivs = np.zeros((8, 8))
    for i in range(8):
        for a in range(8):
            if i != a:
                derivs[i, a] = legend[i] / (legend[a] * (points[i] - points[a]))
    derivs[0, 0] = -14.0
    derivs[7, 7] = 14.0
    return derivs.astype(np.float32), np.asarray(weights, np.float32)


def dot(a, b, dims=((1,), (0,))):
    return lax.dot_general(a, b, (dims, ((), ())), precision=HIGHEST, preferred_element_type=F32)


BF16 = jnp.bfloat16


def narrow(v, terms):
    out = []
    for n in range(terms):
        piece = v.astype(BF16)
        out.append(piece)
        if n < terms - 1:
            v = v - piece.astype(F32)
    return out


def bdot(a, b, dims=((1,), (0,))):
    return lax.dot_general(a, b, (dims, ((), ())), preferred_element_type=F32)


def right(v, pair):
    width = v.shape[1]
    out = bdot(jnp.concatenate(narrow(v, 2), axis=1), pair)
    return out[:, :width] + out[:, width:]


def left(high, low, v):
    width = v.shape[1]
    pieces = narrow(v, 2)
    out = bdot(high, jnp.concatenate(pieces, axis=1))
    return out[:, :width] + out[:, width:] + bdot(low, pieces[0])


def reach(sizes, blocks):
    out = []
    for o in itertools.product(*(range(1 - s, s) for s in sizes)):
        far = sum(max(abs(d) - 1, 0) * b for d, b in zip(o, blocks))
        if far < CHEB_C and o != (0, 0, 0):
            out.append(o)
    return out


def fine_coefficients():
    centre = 0.5 * (FINE_HIGH + FINE_LOW)
    half = 0.5 * (FINE_HIGH - FINE_LOW)
    ratio = centre / half
    rho = 1.0 / ratio
    steps = []
    for _ in range(1, SMOOTH):
        new = 1.0 / (2.0 * ratio - rho)
        steps.append((new * rho, 2.0 * new / half))
        rho = new
    return 1.0 / centre, steps


def kernel(
    sizes,
    blocks,
    temp_hbm,
    flow_hbm,
    cond_hbm,
    vol_hbm,
    off_hbm,
    mats_hbm,
    rows_hbm,
    newt_ref,
    press_ref,
    resid_ref,
    temp_ref,
    flow_ref,
    cond_ref,
    vol_ref,
    off_ref,
    mats_ref,
    rows_ref,
    in_sem,
    weight,
    coef,
    q,
    direc,
    part,
    ysend,
    zsend,
    xrecv,
    yrecv,
    zrecv,
    place,
    csend,
    ctile,
    cgrid,
    padded,
    pz,
    pxy,
    send_sem,
    recv_sem,
    gsend_sem,
    grecv_sem,
):
    derivs, weights = gll_tables()
    nx, ny, nz = sizes
    bx, by, bz = blocks
    lx, ly, lz = 8 * bx, 8 * by, 8 * bz
    rows = 8 * ly
    devices = nx * ny * nz
    grid_x, grid_y, grid_z = nx * bx, ny * by, nz * bz
    ix, iy, iz = lax.axis_index("gx"), lax.axis_index("gy"), lax.axis_index("gz")
    me = (ix * ny + iy) * nz + iz

    loads = [
        pltpu.make_async_copy(a, b, in_sem.at[n])
        for n, (a, b) in enumerate(
            (
                (rows_hbm, rows_ref),
                (off_hbm, off_ref),
                (mats_hbm, mats_ref),
                (temp_hbm, temp_ref),
                (flow_hbm, flow_ref),
                (cond_hbm, cond_ref),
                (vol_hbm, vol_ref),
            )
        )
    ]
    for load in loads:
        load.start()

    xrecv[...] = jnp.zeros(xrecv.shape, F32)
    yrecv[...] = jnp.zeros(yrecv.shape, F32)
    zrecv[...] = jnp.zeros(zrecv.shape, F32)
    place[...] = jnp.zeros(place.shape, F32)
    partners = reach(sizes, blocks)

    def neighbour(o):
        to = (ix + o[0], iy + o[1], iz + o[2])
        there = None
        for value, size, step in zip(to, sizes, o):
            if step:
                ok = (value >= 0) if step < 0 else (value < size)
                there = ok if there is None else (there & ok)
        return to, there

    barrier = pltpu.get_barrier_semaphore()

    met = jnp.int32(0)
    for o in partners:
        to, there = neighbour(o)
        met = met + jnp.where(there, 1, 0)

        @pl.when(there)
        def _():
            pl.semaphore_signal(barrier, inc=1, device_id=to, device_id_type=MESH)

    lane = lax.broadcasted_iota(jnp.int32, (rows, lz), 1)
    row_y = lax.broadcasted_iota(jnp.int32, (rows, lz), 0) % ly
    z_up = (lane % 8 == 7) & (lane < lz - 1)
    z_down = (lane % 8 == 0) & (lane > 0)
    y_up = (row_y % 8 == 7) & (row_y < ly - 1)
    y_down = (row_y % 8 == 0) & (row_y > 0)

    loads[0].wait()
    wyz = rows_ref[0:ly]
    for x in range(lx):
        weight[x] = wyz * float(weights[x % 8])

    def share(node, elements, element):
        owner = node // 8
        local = node % 8
        low = (local == 0) & (owner > 0)
        high = (local == 7) & (owner < elements - 1)
        here = jnp.where(low | high, 0.5, 1.0)
        there = (low & (element == owner - 1)) | (high & (element == owner + 1))
        return jnp.where(element == owner, here, jnp.where(there, 0.5, 0.0))

    pz[...] = share(
        lax.broadcasted_iota(jnp.int32, (128, lz), 1) + iz * lz,
        grid_z,
        lax.broadcasted_iota(jnp.int32, (128, lz), 0),
    ).astype(BF16)
    node = lax.broadcasted_iota(jnp.int32, (lx * ly, grid_x * grid_y), 0)
    elem = lax.broadcasted_iota(jnp.int32, (lx * ly, grid_x * grid_y), 1)
    pxy[...] = (
        share(node // ly + ix * lx, grid_x, elem // grid_y)
        * share(node % ly + iy * ly, grid_y, elem % grid_y)
    ).astype(BF16)
    restr = rows_ref[ly : ly + 128]
    spot = lax.broadcasted_iota(jnp.int32, (8, 128), 1)
    own_row = spot // bz == lax.broadcasted_iota(jnp.int32, (8, 128), 0)
    from_lane = lax.broadcasted_iota(jnp.int32, (128, 128), 0)
    to_lane = lax.broadcasted_iota(jnp.int32, (128, 128), 1)
    fold = jnp.where(from_lane % bz == to_lane % bz, 1.0, 0.0).astype(BF16)

    def along_z(v, n):
        return right(v, mats_ref[n])

    def along_y(v, n):
        return left(mats_ref[3 + n], mats_ref[6 + n], v)

    def along_x(v, matrix):
        layers = [v[a * ly : (a + 1) * ly] for a in range(8)]
        out = []
        for i in range(8):
            acc = layers[0] * float(matrix[i, 0])
            for a in range(1, 8):
                acc = acc + layers[a] * float(matrix[i, a])
            out.append(acc)
        return jnp.concatenate(out, axis=0)

    def block(ref, b, lead=None):
        if lead is None:
            return ref[8 * b : 8 * b + 8].reshape(rows, lz)
        return ref[lead, 8 * b : 8 * b + 8].reshape(rows, lz)

    def assemble_block(v):
        v = (
            v
            + jnp.where(z_up, pltpu.roll(v, lz - 1, 1), 0.0)
            + jnp.where(z_down, pltpu.roll(v, 1, 1), 0.0)
        )
        return (
            v
            + jnp.where(y_up, pltpu.roll(v, rows - 1, 0), 0.0)
            + jnp.where(y_down, pltpu.roll(v, 1, 0), 0.0)
        )

    end_row = lax.broadcasted_iota(jnp.int32, (16, lz), 0)
    end_lane = lax.broadcasted_iota(jnp.int32, (16, lz), 1)
    ends = jnp.where(
        (end_row < 6) & (end_lane == jnp.where(end_row % 2 == 0, 0, lz - 1)), 1.0, 0.0
    ).astype(BF16)
    ends_three = jnp.concatenate([ends] * 3, axis=1)

    def buffers(o, slot):
        ox, oy, oz = o
        if oz:
            out = zsend.at[slot, (oz + 1) // 2]
        elif oy:
            out = ysend.at[slot, (oy + 1) // 2]
        else:
            out = part.at[slot, 0 if ox < 0 else lx - 1]

        def land(p):
            px, py, pz_ = p
            if pz_:
                return zrecv.at[slot, (pz_ + 1) // 2, py + 1, px + 1]
            if py:
                return yrecv.at[slot, (py + 1) // 2, px + 1]
            return xrecv.at[slot, (px + 1) // 2]

        return out, land

    def exists(o):
        return all(s > 1 or not d for s, d in zip(sizes, o))

    def sending(o, slot):
        back = tuple(-d for d in o)
        out, land = buffers(o, slot)
        return pltpu.make_async_remote_copy(
            src_ref=out,
            dst_ref=land(back),
            send_sem=send_sem.at[slot, SLOT_OF[o]],
            recv_sem=recv_sem.at[slot, SLOT_OF[back]],
            device_id=neighbour(o)[0],
            device_id_type=MESH,
        )

    def receiving(o, slot):
        out, land = buffers(o, slot)
        return pltpu.make_async_remote_copy(
            src_ref=out,
            dst_ref=land(o),
            send_sem=send_sem.at[slot, SLOT_OF[o]],
            recv_sem=recv_sem.at[slot, SLOT_OF[o]],
            device_id=neighbour(o)[0],
            device_id_type=MESH,
        )

    def begin(slot, fields):
        if bx == 1:
            part[slot] = fields[0].reshape(lx, ly, lz)
        else:
            for b in range(bx):
                part[slot, 8 * b : 8 * b + 8] = fields[b].reshape(8, ly, lz)
            for b in range(bx - 1):
                both = part[slot, 8 * b + 7] + part[slot, 8 * b + 8]
                part[slot, 8 * b + 7] = both
                part[slot, 8 * b + 8] = both
        ysend[slot, 0] = part[slot, :, 0, :]
        ysend[slot, 1] = part[slot, :, ly - 1, :]
        whole = jnp.concatenate(narrow(part[slot].reshape(lx * ly, lz), 3), axis=1)
        packed = bdot(ends_three, whole, ((1,), (1,)))
        zsend[slot, 0] = packed[0:1]
        zsend[slot, 1] = packed[1:2]
        for o in OFFSETS:
            if exists(o):

                @pl.when(neighbour(o)[1])
                def _():
                    sending(o, slot).start()

    zlane = lax.broadcasted_iota(jnp.int32, (1, lx * ly), 1)

    def finish(slot):
        for o in OFFSETS:
            if exists(o):

                @pl.when(neighbour(o)[1])
                def _():
                    receiving(o, slot).wait()

        span = lx * ly
        gathered = []
        for side in range(2):
            by_y = []
            for cy in range(3):
                acc = zrecv[slot, side, cy, 1]
                if nx > 1:
                    low = pltpu.roll(zrecv[slot, side, cy, 0], ly, 1)
                    high = pltpu.roll(zrecv[slot, side, cy, 2], span - ly, 1)
                    acc = acc + jnp.where(zlane < ly, low, 0.0)
                    acc = acc + jnp.where(zlane >= span - ly, high, 0.0)
                by_y.append(acc)
            acc = by_y[1]
            acc = acc + jnp.where(zlane % ly == 0, pltpu.roll(by_y[0], span - (ly - 1), 1), 0.0)
            acc = acc + jnp.where(zlane % ly == ly - 1, pltpu.roll(by_y[2], ly - 1, 1), 0.0)
            gathered.append(acc)
        pieces = [p.astype(F32) for p in narrow(jnp.concatenate(gathered, axis=0), 3)]
        stacked = jnp.concatenate(pieces + [jnp.zeros((10, span), F32)], axis=0)
        spread = bdot(stacked.astype(BF16), ends, ((0,), (0,)))
        part[slot] = part[slot] + spread.reshape(lx, ly, lz)
        part[slot, 0] = part[slot, 0] + xrecv[slot, 0]
        part[slot, lx - 1] = part[slot, lx - 1] + xrecv[slot, 1]
        for side, at in ((0, 0), (1, ly - 1)):
            part[slot, :, at, :] = part[slot, :, at, :] + yrecv[slot, side, 1]
            part[slot, 0, at : at + 1, :] = (
                part[slot, 0, at : at + 1, :] + yrecv[slot, side, 0, lx - 1 : lx, :]
            )
            part[slot, lx - 1, at : at + 1, :] = (
                part[slot, lx - 1, at : at + 1, :] + yrecv[slot, side, 2, 0:1, :]
            )

    def gather_begin(slot, tile):
        csend[slot] = jnp.sum(jnp.where(own_row, tile, 0.0), axis=0, keepdims=True)
        place[slot, me] = csend[slot]
        for o in partners:
            to, there = neighbour(o)

            @pl.when(there)
            def _():
                gather_copy(slot, o).start()

    def gather_copy(slot, o, arriving=False):
        to, _ = neighbour(o)
        other = (to[0] * ny + to[1]) * nz + to[2]
        return pltpu.make_async_remote_copy(
            src_ref=csend.at[slot],
            dst_ref=place.at[slot, other if arriving else me],
            send_sem=gsend_sem.at[slot, partners.index(o)],
            recv_sem=grecv_sem.at[slot, partners.index(tuple(d if arriving else -d for d in o))],
            device_id=to,
            device_id_type=MESH,
        )

    def gather_finish(slot):
        for o in partners:
            to, there = neighbour(o)

            @pl.when(there)
            def _():
                gather_copy(slot, o, True).wait()

        shape = (devices, 8, 128)
        box_lane = lax.broadcasted_iota(jnp.int32, shape, 2) // bz
        box_row = lax.broadcasted_iota(jnp.int32, shape, 1)
        box_z = lax.broadcasted_iota(jnp.int32, shape, 0) % nz
        boxes = jnp.where(box_lane == box_row, jnp.broadcast_to(place[slot], shape), 0.0)
        boxes = boxes.reshape(devices * 8, 128)
        moved = bdot(jnp.concatenate(narrow(boxes, 3), axis=1), jnp.concatenate([fold] * 3, axis=0))
        moved = jnp.where(box_lane == box_z, moved.reshape(shape), 0.0)
        for gx in range(nx):
            for gy in range(ny):
                at = (gx * ny + gy) * nz
                tile = moved[at]
                for gz in range(1, nz):
                    tile = tile + moved[at + gz]
                for ex in range(bx):
                    cgrid[gx * bx + ex, gy * by : gy * by + by, :] = tile[ex * by : ex * by + by]
        return cgrid[...]

    first = PITERS
    loads[1].wait()
    ctile[...] = jnp.zeros((8, 128), F32)
    for ex in range(bx):
        ctile[ex * by : ex * by + by, 0:bz] = off_ref[ex]
    spread_out = jnp.where((from_lane < bz) & (from_lane == to_lane % bz), 1.0, 0.0).astype(F32)
    off_tile = dot(ctile[...], spread_out)
    for load in loads[2:]:
        load.wait()
    coef[...] = weight[...] * vol_ref[...]

    fields = []
    for b in range(bx):
        t = block(temp_ref, b)
        w = block(weight, b)
        wk = w * block(cond_ref, b)
        tx, ty, tz = along_x(t, derivs), along_y(t, 0), along_z(t, 0)
        advect = block(flow_ref, b, 0) * tx + block(flow_ref, b, 1) * ty
        advect = advect + block(flow_ref, b, 2) * tz
        diffuse = along_x(wk * tx, derivs.T) + along_y(wk * ty, 1) + along_z(wk * tz, 1)
        fields.append(assemble_block(-(w * advect) - diffuse))

    pl.semaphore_wait(barrier, met)
    begin(0, fields)
    gather_begin(first, off_tile)
    fields = []
    squares = (derivs * derivs).T
    for b in range(bx):
        c = block(coef, b)
        jac = along_x(c, squares) + along_y(c, 2) + along_z(c, 2) + HELM_SHIFT * block(weight, b)
        fields.append(assemble_block(jac))
    begin(1, fields)

    def half_if(node_id, count):
        local = node_id % 8
        shared = ((local == 0) & (node_id > 0)) | ((local == 7) & (node_id < count - 1))
        return jnp.where(shared, 0.5, 1.0)

    yz_share = half_if(lax.broadcasted_iota(jnp.int32, (ly, lz), 0) + iy * ly, ny * ly)
    yz_share = yz_share * half_if(lax.broadcasted_iota(jnp.int32, (ly, lz), 1) + iz * lz, nz * lz)
    yz_share = yz_share / wyz * CLOCK_STEP_SIZE

    finish(0)
    for x in range(lx):
        x_share = half_if(jnp.full((ly, lz), x, jnp.int32) + ix * lx, nx * lx)
        scale = yz_share * (x_share * float(1.0 / weights[x % 8]))
        newt_ref[x] = temp_ref[x] + part[0, x] * scale

    fields = []
    for b in range(bx):
        w = block(weight, b)
        out = along_x(w * block(flow_ref, b, 0), derivs.T)
        out = out + along_y(w * block(flow_ref, b, 1), 1)
        out = out + along_z(w * (block(flow_ref, b, 2) + block(newt_ref, b)), 1)
        fields.append(assemble_block(out))
    begin(2, fields)
    finish(1)
    q[...] = 1.0 / part[1]
    shift_c = 6.0 + gather_finish(first)
    padded[...] = jnp.zeros(padded.shape, F32)
    finish(2)
    resid_ref[...] = part[2]
    start, steps = fine_coefficients()
    direc[...] = resid_ref[...] * q[...] * start
    press_ref[...] = direc[...]

    cs = (grid_x, grid_y, 128)
    cinv = 1.0 / shift_c
    cl = lax.broadcasted_iota(jnp.int32, cs, 2)
    c_up = cl < grid_z - 1
    c_down = (cl > 0) & (cl < grid_z)

    def coarse_apply(v):
        padded[1 : grid_x + 1, 8 : 8 + grid_y, :] = v
        beside = padded[0:grid_x, 8 : 8 + grid_y, :] + padded[2 : grid_x + 2, 8 : 8 + grid_y, :]
        beside = beside + padded[1 : grid_x + 1, 7 : 7 + grid_y, :]
        beside = beside + padded[1 : grid_x + 1, 9 : 9 + grid_y, :]
        beside = beside + jnp.where(c_up, pltpu.roll(v, 127, 2), 0.0)
        beside = beside + jnp.where(c_down, pltpu.roll(v, 1, 2), 0.0)
        return shift_c * v - beside

    def coarse_solve(r):
        centre = 0.5 * (COARSE_HIGH + COARSE_LOW)
        half = 0.5 * (COARSE_HIGH - COARSE_LOW)
        ratio = centre / half
        rho = 1.0 / ratio
        d = r * cinv * (1.0 / centre)
        sol = d
        for _ in range(1, CHEB_C):
            r = r - coarse_apply(d)
            new = 1.0 / (2.0 * ratio - rho)
            d = (new * rho) * d + (2.0 * new / half) * (r * cinv)
            sol = sol + d
            rho = new
        return sol

    cycle = SMOOTH + 1
    total = PITERS * cycle

    def step(t, carry):
        k = lax.rem(t, cycle)
        slot = lax.rem(t, 2)
        made = []
        for b in range(bx):
            v = block(direc, b)
            c = block(coef, b)
            out = along_x(c * along_x(v, derivs), derivs.T)
            out = out + along_y(c * along_y(v, 0), 1)
            out = out + along_z(c * along_z(v, 0), 1)
            made.append(assemble_block(out + HELM_SHIFT * block(weight, b) * v))
        begin(slot, made)
        finish(slot)

        @pl.when(k == SMOOTH - 1)
        def _():
            resid_ref[...] = resid_ref[...] - part[slot]
            turn = lax.div(t, cycle)
            sums = []
            for b in range(bx):
                acc = resid_ref[8 * b] * float(weights[0])
                for a in range(1, 8):
                    acc = acc + resid_ref[8 * b + a] * float(weights[a])
                sums.append(acc * rows_ref[ly + 128 : 2 * ly + 128])
            sums = dot(jnp.concatenate(sums, axis=0), restr)
            gather_begin(turn, jnp.sum(sums.reshape(bx * by, 8, 128), axis=1))
            sol = coarse_solve(gather_finish(turn)).reshape(grid_x * grid_y, 128)
            count = grid_x * grid_y
            along = bdot(jnp.concatenate(narrow(sol, 3), axis=0), pz[...])
            along = along[0:count] + along[count : 2 * count] + along[2 * count :]
            wide = bdot(pxy[...], jnp.concatenate(narrow(along, 3), axis=1))
            wide = wide[:, 0:lz] + wide[:, lz : 2 * lz] + wide[:, 2 * lz :]
            wide = wide.reshape(lx, ly, lz)
            for x in range(lx):
                direc[x] = wide[x]
                press_ref[x] = press_ref[x] + wide[x]

        @pl.when(k != SMOOTH - 1)
        def _():
            alpha = jnp.float32(0.0)
            beta = jnp.float32(start)
            for n, (a, b) in enumerate(steps):
                alpha = jnp.where(k == n, jnp.float32(a), alpha)
                beta = jnp.where(k == n, jnp.float32(b), beta)
            taken = jnp.where(t < total - 1, jnp.float32(1.0), jnp.float32(0.0))
            for x in range(lx):
                r = resid_ref[x] - part[slot, x]
                resid_ref[x] = r
                d = alpha * direc[x] + beta * (r * q[x])
                direc[x] = d
                press_ref[x] = press_ref[x] + taken * d

        return carry

    lax.fori_loop(0, total, step, 0)


def shards(sizes, temp, flow, cond, vol, off):
    derivs, weights = gll_tables()
    lx, ly, lz = temp.shape
    blocks = off.shape
    bx, by, bz = blocks
    devices = sizes[0] * sizes[1] * sizes[2]
    squares = derivs * derivs
    eye_z = np.eye(bz, dtype=np.float32)
    eye_y = np.eye(ly, dtype=np.float32)

    def halves(m):
        high = m.astype(BF16)
        return high, (m - high.astype(np.float32)).astype(BF16)

    mats = np.zeros((9, 8 * ly, 8 * ly), BF16)
    for n, m in enumerate((derivs.T, derivs, squares)):
        high, low = halves(np.kron(eye_z, m))
        mats[n, :lz, :lz] = high
        mats[n, :lz, lz:] = low
        mats[n, lz:, :lz] = high
        mats[3 + n], mats[6 + n] = halves(np.kron(eye_y, m.T))
    w_y, w_z = np.tile(weights, by), np.tile(weights, bz)
    wyz = w_y[:, None] * w_z[None, :]
    lanes = np.arange(128)[None, :] % bz == np.arange(lz)[:, None] // 8
    restr = np.where(lanes, w_z[:, None] * np.float32(0.125), np.float32(0.0))
    wy_rows = np.broadcast_to(w_y[:, None], (ly, 128))
    table = np.concatenate([wyz, restr, wy_rows], axis=0).astype(np.float32)
    cube = jax.ShapeDtypeStruct((lx, ly, lz), jnp.float32)
    vmem = pl.BlockSpec(memory_space=pltpu.VMEM)
    grid = (sizes[0] * bx, sizes[1] * by)
    hbm = pl.BlockSpec(memory_space=pl.ANY)
    span = len(reach(sizes, blocks))
    scratch = [
        pltpu.VMEM((lx, ly, lz), F32),
        pltpu.VMEM((3, lx, ly, lz), F32),
        pltpu.VMEM((lx, ly, lz), F32),
        pltpu.VMEM((lx, ly, lz), F32),
        pltpu.VMEM(blocks, F32),
        pltpu.VMEM(mats.shape, BF16),
        pltpu.VMEM(table.shape, F32),
        pltpu.SemaphoreType.DMA((7,)),
        pltpu.VMEM((lx, ly, lz), F32),
        pltpu.VMEM((lx, ly, lz), F32),
        pltpu.VMEM((lx, ly, lz), F32),
        pltpu.VMEM((lx, ly, lz), F32),
        pltpu.VMEM((3, lx, ly, lz), F32),
        pltpu.VMEM((3, 2, lx, lz), F32),
        pltpu.VMEM((3, 2, 1, lx * ly), F32),
        pltpu.VMEM((3, 2, ly, lz), F32),
        pltpu.VMEM((3, 2, 3, lx, lz), F32),
        pltpu.VMEM((3, 2, 3, 3, 1, lx * ly), F32),
        pltpu.VMEM((PITERS + 1, devices, 1, 128), F32),
        pltpu.VMEM((PITERS + 1, 1, 128), F32),
        pltpu.VMEM((8, 128), F32),
        pltpu.VMEM((grid[0], grid[1], 128), F32),
        pltpu.VMEM((grid[0] + 2, grid[1] + 16, 128), F32),
        pltpu.VMEM((128, lz), BF16),
        pltpu.VMEM((lx * ly, grid[0] * grid[1]), BF16),
        pltpu.SemaphoreType.DMA((3, len(OFFSETS))),
        pltpu.SemaphoreType.DMA((3, len(OFFSETS))),
        pltpu.SemaphoreType.DMA((PITERS + 1, span)),
        pltpu.SemaphoreType.DMA((PITERS + 1, span)),
    ]
    return pl.pallas_call(
        functools.partial(kernel, sizes, blocks),
        out_shape=(cube, cube, cube),
        in_specs=[hbm] * 7,
        out_specs=(vmem, vmem, vmem),
        scratch_shapes=scratch,
        compiler_params=pltpu.CompilerParams(
            collective_id=0, has_side_effects=True, vmem_limit_bytes=62 * 1024 * 1024
        ),
        name="spectral_step",
    )(temp, flow, cond, vol, off, jnp.asarray(mats), jnp.asarray(table))


def solution(mesh):
    cube = P("gx", "gy", "gz")
    sizes = tuple(mesh.shape[name] for name in ("gx", "gy", "gz"))
    return jax.shard_map(
        functools.partial(shards, sizes),
        mesh=mesh,
        in_specs=(cube, P(None, "gx", "gy", "gz"), cube, cube, cube),
        out_specs=(cube, cube, cube),
        check_vma=False,
    )
```
